1024 devices in a mesh: row: 32 (over x, z_hi, core), col: 32 (over z_lo, y).
Axes of the slice: x: 8, y: 8, z: 8 (z_hi: 2, z_lo: 4; z = z_hi * 4 + z_lo), core: 2. Of those that a mesh axis runs over, the one named last changes fastest.
Arguments:
- a_blocks: float32 [32, 32, 3, 256, 256], P('row', 'col'), may hold values from -1.5 to 1.5
- a_positions: int32 [32, 32, 3], P('row', 'col'), may hold values from 0 to 4, as said below
- b_blocks: float32 [32, 32, 3, 256, 256], P('row', 'col'), may hold values from -1.5 to 1.5
- b_positions: int32 [32, 32, 3], P('row', 'col'), may hold values from 0 to 4, as said below
Outputs:
- product: float32 [16384, 16384], P('row', 'col')
The draws below stay inside these ranges and needn't reach their ends.
Inputs may be any that keep to these rules, and one draw needn't show every extreme that they name: `a_positions`: in each device's list the filled slots come first and name distinct tile positions; the value 2 * 2 marks an empty slot; every device has one filled slot or more, some device has all 3 filled and some device exactly one. `b_positions`: as for a_positions.
All inputs are finite; a program needn't handle non-finite values.
Results may differ from the reference program's by a relative error of at most 0.0003.
Values sent between devices are 32-bit elements; how exact they have to be, the bound alone decides.
A program may use at most 32 MiB of HBM per device.

```python
import jax
import jax.numpy as jnp
from jax import lax

BLK = 256
TB = 2
SLOTS = 3
N_ROW = 32
N_COL = 32


def pattern(key):
    cells = TB * TB
    first, second = jax.random.split(key)
    scores = jax.random.randint(first, (N_ROW, N_COL, cells), 0, 1 << 20) * cells + jnp.arange(cells, dtype=jnp.int32)
    order = jnp.argsort(scores, axis=-1)[..., :SLOTS].astype(jnp.int32)
    counts = jax.random.randint(second, (N_ROW * N_COL,), 1, SLOTS + 1)
    counts = counts.at[0].set(SLOTS).at[1].set(1).reshape(N_ROW, N_COL)
    slot_ids = jnp.arange(SLOTS, dtype=jnp.int32)
    return jnp.where(slot_ids < counts[..., None], order, cells).astype(jnp.int32)


def draw_a_positions(key, part):
    key = jax.random.fold_in(key, 11)
    return pattern(key)


def draw_b_positions(key, part):
    key = jax.random.fold_in(key, 23)
    return pattern(key)


def shard_levels(rng, shape, cuts, low, largest):
    gain = 1.0
    for position, blocks in cuts:
        steps = jax.random.uniform(jax.random.fold_in(jax.random.fold_in(rng, 6), position), (blocks,), jnp.float32, low / len(cuts), largest / len(cuts))
        gain = gain * jnp.repeat(jnp.exp(steps), shape[position] // blocks).reshape((-1,) + (1,) * (len(shape) - 1 - position))
    return gain


def bell_draw(stream_key, extent, width, most, shards=(), held_as=jnp.bfloat16):
    drawn = width * jax.random.normal(stream_key, extent, jnp.float32)
    if shards:
        drawn = drawn * shard_levels(stream_key, extent, shards, -0.22, 0.18)
    return jnp.clip(drawn, -most, most).astype(held_as)


def setup_inputs(seed: int = 0) -> dict:
    seeds = jax.random.split(jax.random.key(seed), 5)
    return {
        "a_blocks": bell_draw(seeds[0], (N_ROW, N_COL, SLOTS, BLK, BLK), 0.25, 1.5, ((0, 32), (1, 32)), jnp.float32),
        "a_positions": draw_a_positions(jax.random.fold_in(seeds[4], 71), 0),
        "b_blocks": bell_draw(seeds[2], (N_ROW, N_COL, SLOTS, BLK, BLK), 0.25, 1.5, ((0, 32), (1, 32)), jnp.float32),
        "b_positions": draw_b_positions(jax.random.fold_in(seeds[4], 71), 0),
    }


def densify(blocks, positions):
    cells = TB * TB
    onehot = (positions[..., None] == jnp.arange(cells, dtype=jnp.int32)).astype(jnp.float32)
    tiles = jnp.einsum('sp,sxy->pxy', onehot, blocks.astype(jnp.float32), precision=lax.Precision.HIGHEST)
    tiles = tiles.reshape(TB, TB, BLK, BLK).transpose(0, 2, 1, 3)
    return tiles.reshape(TB * BLK, TB * BLK)


def dense_row(blocks, positions):
    return jax.vmap(densify)(blocks, positions)


def matmul(left, right):
    return jnp.dot(left, right, precision=lax.Precision.HIGHEST, preferred_element_type=jnp.float32)


def reference(a_blocks, a_positions, b_blocks, b_positions):
    def one_row(index):
        lower = (index + 1) % N_ROW
        a_tiles = dense_row(a_blocks[index], a_positions[index])
        b_tiles = dense_row(b_blocks[index], b_positions[index])
        b_lower = dense_row(b_blocks[lower], b_positions[lower])
        a_next = jnp.roll(a_tiles, -1, axis=0)
        terms = jax.vmap(matmul)(a_tiles, b_tiles) + jax.vmap(matmul)(a_next, b_lower)
        return terms.transpose(1, 0, 2).reshape(TB * BLK, N_COL * TB * BLK)

    rows = lax.map(one_row, jnp.arange(N_ROW, dtype=jnp.int32))
    return rows.reshape(N_ROW * TB * BLK, N_COL * TB * BLK)
```

```python
import jax
import jax.numpy as jnp
from jax import lax
from jax.experimental import pallas as pl
from jax.experimental.pallas import tpu as pltpu
from jax.sharding import PartitionSpec as P

BLK = 256
TB = 2
SLOTS = 3
SIDE = BLK * TB
MESH = pl.DeviceIdType.MESH


def place():
    r, c = lax.axis_index("row"), lax.axis_index("col")
    return r // 4, c % 8, (r // 2) % 2 * 4 + c // 8, r % 2


def device(x, y, z, core):
    x, y, z = (v % 8 for v in (x, y, z))
    return (x * 4 + z // 4 * 2 + core, z % 4 * 8 + y)


def along(rows, cols):
    r, c = lax.axis_index("row"), lax.axis_index("col")
    return ((r + rows) % 32, (c + cols) % 32)


def signal(sem, target):
    pl.semaphore_signal(sem, inc=1, device_id=target, device_id_type=MESH)


def densify(slots, where, high, low):
    positions = where[...]
    for p in range(TB * TB):
        r, k = p // TB, p % TB
        chosen = [(positions[:, s : s + 1] == p).astype(jnp.float32) for s in range(SLOTS)]
        block = chosen[0] * slots[0] + chosen[1] * slots[1] + chosen[2] * slots[2]
        top = block.astype(jnp.bfloat16)
        rest = (block - top.astype(jnp.float32)).astype(jnp.bfloat16)
        spot = (pl.ds(r * BLK, BLK), pl.ds(k * BLK, BLK))
        high[spot] = top
        low[spot] = rest


def product(left, right, c):
    cols = pl.ds(c * BLK, BLK)
    (lh, ll), (rh, rl) = left, right

    def dot(u, v):
        return jnp.dot(u, v, preferred_element_type=jnp.float32)

    return dot(lh[...], rh[:, cols]) + dot(lh[...], rl[:, cols]) + dot(ll[...], rh[:, cols])


def kernel(a, a_pos, b, b_pos, out, a_own, b_own, a_in, b_in, where, tiles, load, send, recv, ready):
    x, y, z, core = place()
    far = core == 0
    upper = z >= 4
    barrier = pltpu.get_barrier_semaphore()

    local = [
        pltpu.make_async_copy(a, a_own, load.at[0]),
        pltpu.make_async_copy(b, b_own, load.at[1]),
        pltpu.make_async_copy(a_pos, where.at[0], load.at[2]),
        pltpu.make_async_copy(b_pos, where.at[1], load.at[3]),
    ]
    for copy in local:
        copy.start()

    a_to, a_from = along(0, -1), along(0, 1)
    b_to, b_from = along(-1, 0), along(1, 0)

    def outgoing(src, dst, which, slot, target):
        return pltpu.make_async_remote_copy(
            src_ref=src,
            dst_ref=dst,
            send_sem=send.at[which, slot],
            recv_sem=recv.at[which, slot],
            device_id=target,
            device_id_type=MESH,
        )

    a_sends = [outgoing(a_pos, where.at[2], 0, SLOTS, a_to)]
    a_sends += [outgoing(a.at[s], a_in.at[s], 0, s, a_to) for s in range(SLOTS)]
    b_sends = [outgoing(b_pos, where.at[3], 1, SLOTS, b_to)]
    b_sends += [outgoing(b.at[s], b_in.at[s], 1, s, b_to) for s in range(SLOTS)]

    def start(copies):
        for copy in copies:
            copy.start()

    signal(barrier, a_from)

    @pl.when(far)
    def _():
        @pl.when(jnp.logical_not(upper))
        def _():
            signal(barrier, b_to)
            pl.semaphore_wait(barrier, 2)

        @pl.when(upper)
        def _():
            pl.semaphore_wait(barrier, 3)

        signal(ready, b_from)
        start(a_sends)

        @pl.when(upper)
        def _():
            start(b_sends)

    @pl.when(jnp.logical_not(far))
    def _():
        signal(barrier, b_to)

        @pl.when(jnp.logical_not(upper))
        def _():
            signal(barrier, b_from)
            pl.semaphore_wait(barrier, 1)

        @pl.when(upper)
        def _():
            pl.semaphore_wait(barrier, 2)
            signal(ready, b_from)

        start(a_sends)
        pl.semaphore_wait(ready, 1)
        start(b_sends)

    for copy in local:
        copy.wait()
    ah, al, bh, bl = (tiles.at[i] for i in range(4))
    densify(a_own, where.at[0], ah, al)
    densify(b_own, where.at[1], bh, bl)
    for c in range(TB):
        out[:, pl.ds(c * BLK, BLK)] = product((ah, al), (bh, bl), c)

    @pl.when(jnp.logical_and(far, jnp.logical_not(upper)))
    def _():
        pl.semaphore_wait(ready, 1)
        start(b_sends)

    for copy in a_sends:
        copy.wait_recv()
    densify(a_in, where.at[2], ah, al)
    for copy in b_sends:
        copy.wait_recv()
    densify(b_in, where.at[3], bh, bl)
    for c in range(TB):
        out[:, pl.ds(c * BLK, BLK)] += product((ah, al), (bh, bl), c)
    for copy in a_sends + b_sends:
        copy.wait_send()


def body(a_blocks, a_positions, b_blocks, b_positions):
    held = pltpu.VMEM((SLOTS, BLK, BLK), jnp.float32)
    return pl.pallas_call(
        kernel,
        out_shape=jax.ShapeDtypeStruct((SIDE, SIDE), jnp.float32),
        in_specs=[pl.BlockSpec(memory_space=pltpu.HBM)] * 4,
        out_specs=pl.BlockSpec(memory_space=pltpu.VMEM),
        scratch_shapes=[
            held,
            held,
            held,
            held,
            pltpu.VMEM((4, 1, SLOTS), jnp.int32),
            pltpu.VMEM((4, SIDE, SIDE), jnp.bfloat16),
            pltpu.SemaphoreType.DMA((4,)),
            pltpu.SemaphoreType.DMA((2, SLOTS + 1)),
            pltpu.SemaphoreType.DMA((2, SLOTS + 1)),
            pltpu.SemaphoreType.REGULAR,
        ],
        compiler_params=pltpu.CompilerParams(
            collective_id=0, has_side_effects=True, vmem_limit_bytes=40 * 1024 * 1024
        ),
    )(a_blocks[0, 0], a_positions[0], b_blocks[0, 0], b_positions[0])


def solution(mesh):
    placed = (
        P("row", "col", None, None, None),
        P("row", "col", None),
        P("row", "col", None, None, None),
        P("row", "col", None),
    )
    return jax.shard_map(body, mesh=mesh, in_specs=placed, out_specs=P("row", "col"), check_vma=False)
```

```python
import jax
import jax.numpy as jnp
from jax import lax
from jax.experimental import pallas as pl
from jax.experimental.pallas import tpu as pltpu
from jax.sharding import PartitionSpec as P

BLK = 256
TB = 2
SLOTS = 3
SIDE = BLK * TB
MESH = pl.DeviceIdType.MESH


def place():
    r, c = lax.axis_index("row"), lax.axis_index("col")
    return r // 4, c % 8, (r // 2) % 2 * 4 + c // 8, r % 2


def device(x, y, z, core):
    return (x * 4 + z // 4 * 2 + core, z % 4 * 8 + y)


def along(rows, cols):
    r, c = lax.axis_index("row"), lax.axis_index("col")
    return ((r + rows) % 32, (c + cols) % 32)


def signal(sem, target):
    pl.semaphore_signal(sem, inc=1, device_id=target, device_id_type=MESH)


def start(copies):
    for copy in copies:
        copy.start()


def halves(block):
    top = block.astype(jnp.bfloat16)
    return top, (block - top.astype(jnp.float32)).astype(jnp.bfloat16)


def densify(slots, where, high, low):
    positions = where[...]
    for p in range(TB * TB):
        r, k = p // TB, p % TB
        chosen = [(positions[:, s : s + 1] == p).astype(jnp.float32) for s in range(SLOTS)]
        block = chosen[0] * slots[0] + chosen[1] * slots[1] + chosen[2] * slots[2]
        spot = (pl.ds(r * BLK, BLK), pl.ds(k * BLK, BLK))
        high[spot], low[spot] = halves(block)


def three_dots(lh, ll, rh, rl):
    def dot(u, v):
        return jnp.dot(u, v, preferred_element_type=jnp.float32)

    return dot(lh, rh) + dot(lh, rl) + dot(ll, rh)


def kernel(
    a, a_pos, b, b_pos, out, a_own, b_own, a_in, b_in, passing, where, tiles, load, send, recv, relay, ready, ready_wrap, ready_last
):
    x, y, z, core = place()
    lo = z % 4
    far = core == 0
    upper = z >= 4
    barrier = pltpu.get_barrier_semaphore()

    local = [
        pltpu.make_async_copy(a, a_own, load.at[0]),
        pltpu.make_async_copy(b, b_own, load.at[1]),
        pltpu.make_async_copy(a_pos, where.at[0], load.at[2]),
        pltpu.make_async_copy(b_pos, where.at[1], load.at[3]),
    ]
    start(local)

    wrap = y == 0
    detour = jnp.where(far, 1, 6)
    aside = y == detour
    onward = jnp.logical_or(wrap, aside)
    arriving = jnp.logical_or(onward, y == 7)
    z_to = jnp.where(lo == 0, z + 3, z - 1)
    z_from = jnp.where(lo == 3, z - 3, z + 1)
    wrap_to = [device(x, 7, z_to, core), device(x, 0, z_to, core), device(x, detour, z_to, core)]
    wrap_from = device(x, 0, z_from, core)
    last = device(x, 7, z, core)
    a_to, a_from = along(0, -1), along(0, 1)
    b_to, b_from = along(-1, 0), along(1, 0)

    def remote(src, dst, ss, rs, target):
        return pltpu.make_async_remote_copy(
            src_ref=src, dst_ref=dst, send_sem=ss, recv_sem=rs, device_id=target, device_id_type=MESH
        )

    def to_slot(src, which, slot, target):
        dst = (a_in, b_in)[which].at[slot]
        return remote(src, dst, send.at[which, slot], recv.at[which, slot], target)

    a_places = remote(a_pos, where.at[2], send.at[0, SLOTS], recv.at[0, SLOTS], a_to)
    b_places = remote(b_pos, where.at[3], send.at[1, SLOTS], recv.at[1, SLOTS], b_to)
    a_sends = [to_slot(a.at[s], 0, s, a_to) for s in range(SLOTS)]
    b_sends = [to_slot(b.at[s], 1, s, b_to) for s in range(SLOTS)]
    step = [remote(a.at[s], passing, send.at[0, s], relay.at[0], wrap_to[s]) for s in (1, 2)]
    slot = jnp.where(wrap, 1, 2)
    forward = remote(passing, a_in.at[slot], relay.at[1], recv.at[0, slot], last)

    def send_wrapped():
        a_places.start()
        start(step)
        a_sends[0].start()

    late = lo == 3

    @pl.when(y < 7)
    def _():
        signal(barrier, a_from)

    @pl.when(jnp.logical_and(arriving, jnp.logical_not(late)))
    def _():
        signal(barrier, wrap_from)

    @pl.when(jnp.logical_and(wrap, lo == 0))
    def _():
        for target in wrap_to:
            signal(barrier, target)

    @pl.when(jnp.logical_or(wrap, jnp.logical_and(y == 1, far)))
    def _():
        signal(barrier, last)

    @pl.when(jnp.logical_or(jnp.logical_not(far), jnp.logical_not(upper)))
    def _():
        signal(barrier, b_to)

    @pl.when(jnp.logical_and(jnp.logical_not(far), jnp.logical_not(upper)))
    def _():
        signal(barrier, b_from)

    def count(condition, number=1):
        return jnp.where(condition, number, 0)

    need = count(y > 0) + count(jnp.logical_and(wrap, lo > 0), 3) + count(far) + count(upper)
    need += count(y == 7, 1 + count(far)) + count(jnp.logical_and(arriving, late))

    @pl.when(need > 0)
    def _():
        pl.semaphore_wait(barrier, need)

    @pl.when(jnp.logical_or(far, upper))
    def _():
        signal(ready, b_from)

    @pl.when(jnp.logical_and(far, upper))
    def _():
        b_places.start()
        start(b_sends)

    @pl.when(jnp.logical_and(arriving, late))
    def _():
        signal(ready_wrap, wrap_from)

    @pl.when(y == 7)
    def _():
        signal(ready_last, device(x, 0, z, core))
        signal(ready_last, device(x, detour, z, core))

    @pl.when(y > 0)
    def _():
        a_places.start()
        start(a_sends)

    @pl.when(jnp.logical_and(wrap, lo > 0))
    def _():
        send_wrapped()

    @pl.when(jnp.logical_not(far))
    def _():
        pl.semaphore_wait(ready, 1)
        b_places.start()
        start(b_sends)

    for copy in local:
        copy.wait()
    ah, al, bh, bl = (tiles.at[i] for i in range(4))
    densify(a_own, where.at[0], ah, al)
    densify(b_own, where.at[1], bh, bl)
    for c in range(TB):
        cols = pl.ds(c * BLK, BLK)
        out[:, cols] = three_dots(ah[...], al[...], bh[:, cols], bl[:, cols])

    @pl.when(jnp.logical_and(wrap, lo == 0))
    def _():
        pl.semaphore_wait(ready_wrap, SLOTS)
        send_wrapped()

    @pl.when(jnp.logical_and(far, jnp.logical_not(upper)))
    def _():
        pl.semaphore_wait(ready, 1)
        b_places.start()
        start(b_sends)

    @pl.when(onward)
    def _():
        pl.semaphore_wait(ready_last, 1)
        step[0].wait_recv()
        forward.start()

    for copy in [a_places] + a_sends:
        copy.wait_recv()
    densify(a_in, where.at[2], ah, al)
    b_places.wait_recv()
    positions = where[3]
    for s in range(SLOTS):
        row = positions[:, s : s + 1] // TB
        picked = [jnp.where(row == 0, t[:, :BLK], jnp.where(row == 1, t[:, BLK:], 0)) for t in (ah[...], al[...])]
        b_sends[s].wait_recv()
        term = three_dots(*picked, *halves(b_in[s]))
        for c in range(TB):
            here = jnp.logical_and(positions[:, s : s + 1] % TB == c, row < TB).astype(jnp.float32)
            out[:, pl.ds(c * BLK, BLK)] += here * term

    for copy in [a_places, b_places] + a_sends + b_sends:
        copy.wait_send()

    @pl.when(onward)
    def _():
        forward.wait_send()


def body(a_blocks, a_positions, b_blocks, b_positions):
    held = pltpu.VMEM((SLOTS, BLK, BLK), jnp.float32)
    inputs = (a_blocks[0, 0], a_positions[0], b_blocks[0, 0], b_positions[0])
    return pl.pallas_call(
        kernel,
        out_shape=jax.ShapeDtypeStruct((SIDE, SIDE), jnp.float32),
        in_specs=[pl.BlockSpec(memory_space=pltpu.HBM)] * 4,
        out_specs=pl.BlockSpec(memory_space=pltpu.VMEM),
        scratch_shapes=[
            held,
            held,
            held,
            held,
            pltpu.VMEM((BLK, BLK), jnp.float32),
            pltpu.VMEM((4, 1, SLOTS), jnp.int32),
            pltpu.VMEM((4, SIDE, SIDE), jnp.bfloat16),
            pltpu.SemaphoreType.DMA((4,)),
            pltpu.SemaphoreType.DMA((2, SLOTS + 1)),
            pltpu.SemaphoreType.DMA((2, SLOTS + 1)),
            pltpu.SemaphoreType.DMA((2,)),
            pltpu.SemaphoreType.REGULAR,
            pltpu.SemaphoreType.REGULAR,
            pltpu.SemaphoreType.REGULAR,
        ],
        compiler_params=pltpu.CompilerParams(
            collective_id=0, has_side_effects=True, vmem_limit_bytes=40 * 1024 * 1024
        ),
    )(*(pltpu.with_memory_space_constraint(v, pltpu.HBM) for v in inputs))


def solution(mesh):
    placed = (
        P("row", "col", None, None, None),
        P("row", "col", None),
        P("row", "col", None, None, None),
        P("row", "col", None),
    )
    return jax.shard_map(body, mesh=mesh, in_specs=placed, out_specs=P("row", "col"), check_vma=False)
```

```python
import jax
import jax.numpy as jnp
from jax import lax
from jax.experimental import pallas as pl
from jax.experimental.pallas import tpu as pltpu
from jax.sharding import PartitionSpec as P

BLK = 256
TB = 2
SLOTS = 3
SIDE = BLK * TB
PARTS = 2
MESH = pl.DeviceIdType.MESH


def place():
    r, c = lax.axis_index("row"), lax.axis_index("col")
    return r // 4, c % 8, (r // 2) % 2 * 4 + c // 8, r % 2


def device(x, y, z, core):
    return (x * 4 + z // 4 * 2 + core, z % 4 * 8 + y)


def along(rows, cols):
    r, c = lax.axis_index("row"), lax.axis_index("col")
    return ((r + rows) % 32, (c + cols) % 32)


def signal(sem, target):
    pl.semaphore_signal(sem, inc=1, device_id=target, device_id_type=MESH)


def start(copies):
    for copy in copies:
        copy.start()


def halves(block):
    top = block.astype(jnp.bfloat16)
    return top, (block - top.astype(jnp.float32)).astype(jnp.bfloat16)


def densify(slots, where, high, low):
    positions = where[...]
    for p in range(TB * TB):
        r, k = p // TB, p % TB
        chosen = [(positions[:, s : s + 1] == p).astype(jnp.float32) for s in range(SLOTS)]
        block = chosen[0] * slots[0] + chosen[1] * slots[1] + chosen[2] * slots[2]
        spot = (pl.ds(r * BLK, BLK), pl.ds(k * BLK, BLK))
        high[spot], low[spot] = halves(block)


def three_dots(lh, ll, rh, rl):
    def dot(u, v):
        return jnp.dot(u, v, preferred_element_type=jnp.float32)

    return dot(lh, rh) + dot(lh, rl) + dot(ll, rh)


def kernel(
    a, a_pos, b, b_pos, out, a_own, b_own, a_in, b_in, passing, where, tiles, load, send, recv, relay, ready, ready_wrap, ready_last, ready_over
):
    x, y, z, core = place()
    lo = z % 4
    far = core == 0
    upper = z >= 4
    barrier = pltpu.get_barrier_semaphore()

    local = [
        pltpu.make_async_copy(a, a_own, load.at[0]),
        pltpu.make_async_copy(b, b_own, load.at[1]),
        pltpu.make_async_copy(a_pos, where.at[0], load.at[2]),
        pltpu.make_async_copy(b_pos, where.at[1], load.at[3]),
    ]
    start(local)

    wrap = y == 0
    detour = jnp.where(far, 1, 2)
    aside = y == detour
    inner = jnp.logical_or(wrap, aside)
    outer = y == 7
    lower = jnp.logical_not(upper)
    near = jnp.logical_not(far)
    early, late = lo == 0, lo == 3
    first, second = z == 0, z == 1
    told = jnp.logical_and(wrap, first)
    z_to = jnp.where(early, z + 3, z - 1)
    z_from = jnp.where(late, z - 3, z + 1)
    wrap_to = [device(x, 7, z, core), device(x, 0, z_to, core), device(x, detour, z_to, core)]
    wrap_from = device(x, 0, z_from, core)
    last = device(x, 7, z, core)
    last_to, last_from = device(x, 7, z_to, core), device(x, 7, z_from, core)
    a_to, a_from = along(0, -1), along(0, 1)
    b_to, b_from = along(-1, 0), along(1, 0)

    def remote(src, dst, ss, rs, target):
        return pltpu.make_async_remote_copy(
            src_ref=src, dst_ref=dst, send_sem=ss, recv_sem=rs, device_id=target, device_id_type=MESH
        )

    def to_slot(src, which, slot, target):
        dst = (a_in, b_in)[which].at[slot]
        return remote(src, dst, send.at[which, slot], recv.at[which, slot], target)

    a_places = remote(a_pos, where.at[2], send.at[0, SLOTS], recv.at[0, SLOTS], a_to)
    b_places = remote(b_pos, where.at[3], send.at[1, SLOTS], recv.at[1, SLOTS], b_to)
    a_sends = [to_slot(a.at[s], 0, s, a_to) for s in range(SLOTS)]
    b_sends = [to_slot(b.at[s], 1, s, b_to) for s in range(SLOTS)]

    rows = [pl.ds(i * BLK // PARTS, BLK // PARTS) for i in range(PARTS)]
    step_places = remote(a_pos, where.at[4], send.at[0, SLOTS], relay.at[2, 0], wrap_to[0])
    step = [
        [remote(a.at[s, part], passing.at[part], send.at[0, s], relay.at[0, i], wrap_to[s]) for i, part in enumerate(rows)]
        for s in range(SLOTS)
    ]
    slot = jnp.where(outer, 0, jnp.where(wrap, 1, 2))
    target = [jnp.where(outer, u, v) for u, v in zip(last_to, last)]
    pass_places = remote(where.at[4], where.at[2], relay.at[2, 1], recv.at[0, SLOTS], tuple(target))
    forward = [
        remote(passing.at[part], a_in.at[slot, part], relay.at[1, i], recv.at[0, slot], tuple(target))
        for i, part in enumerate(rows)
    ]

    @pl.when(y < 7)
    def _():
        signal(barrier, a_from)

    @pl.when(jnp.logical_and(inner, jnp.logical_not(jnp.logical_or(late, told))))
    def _():
        signal(barrier, wrap_from)

    @pl.when(jnp.logical_and(wrap, jnp.logical_or(early, second)))
    def _():
        signal(barrier, wrap_to[1])

    @pl.when(jnp.logical_and(wrap, early))
    def _():
        signal(barrier, wrap_to[2])

    @pl.when(jnp.logical_and(wrap, jnp.logical_not(early)))
    def _():
        signal(barrier, last_to)

    @pl.when(jnp.logical_and(outer, early))
    def _():
        signal(barrier, last_to)

    @pl.when(jnp.logical_and(inner, jnp.logical_not(told)))
    def _():
        signal(barrier, last)

    @pl.when(jnp.logical_and(outer, first))
    def _():
        signal(barrier, device(x, 0, z, core))

    @pl.when(jnp.logical_or(near, lower))
    def _():
        signal(barrier, b_to)

    @pl.when(jnp.logical_and(near, lower))
    def _():
        signal(barrier, b_from)

    def count(condition, number=1):
        return jnp.where(condition, number, 0)

    need = count(y > 0) + count(jnp.logical_and(wrap, jnp.logical_not(early)), 2 - count(second))
    need += count(far) + count(upper) + count(outer, 3 - count(first)) + count(told, 2)
    need += count(jnp.logical_and(inner, late))

    @pl.when(need > 0)
    def _():
        pl.semaphore_wait(barrier, need)

    @pl.when(jnp.logical_or(far, upper))
    def _():
        signal(ready, b_from)

    @pl.when(jnp.logical_and(far, upper))
    def _():
        b_places.start()
        start(b_sends)

    @pl.when(jnp.logical_or(jnp.logical_and(wrap, late), told))
    def _():
        signal(ready_wrap, wrap_from)

    @pl.when(jnp.logical_and(aside, late))
    def _():
        signal(ready_over, wrap_from)

    @pl.when(outer)
    def _():
        @pl.when(z > 0)
        def _():
            signal(ready_last, device(x, 0, z, core))

        signal(ready_last, device(x, detour, z, core))

        @pl.when(late)
        def _():
            signal(ready_wrap, last_from)

        @pl.when(jnp.logical_not(late))
        def _():
            signal(ready_over, wrap_from)

    @pl.when(y > 0)
    def _():
        a_places.start()
        start(a_sends)

    @pl.when(jnp.logical_and(wrap, jnp.logical_not(early)))
    def _():
        @pl.when(jnp.logical_not(second))
        def _():
            start(step[1])

        start(step[2])
        pl.semaphore_wait(ready_over, 1)
        a_places.start()
        a_sends[0].start()

        @pl.when(second)
        def _():
            pl.semaphore_wait(ready_wrap, 1)
            start(step[1])

    @pl.when(jnp.logical_and(wrap, early))
    def _():
        @pl.when(z > 0)
        def _():
            pl.semaphore_wait(ready_last, 1)

        step_places.start()
        start(step[0])
        pl.semaphore_wait(ready_wrap, 1)
        start(step[1])
        pl.semaphore_wait(ready_over, 1)
        start(step[2])

    @pl.when(near)
    def _():
        pl.semaphore_wait(ready, 1)
        b_places.start()
        start(b_sends)

    def pass_on():
        for one, other in zip(step[0], forward):
            one.wait_recv()
            other.start()

    @pl.when(jnp.logical_and(outer, early))
    def _():
        pl.semaphore_wait(ready_wrap, 1)
        step_places.wait_recv()
        pass_places.start()
        pass_on()

    held_up = jnp.logical_and(jnp.logical_and(far, lower), jnp.logical_and(z >= 2, jnp.logical_and(y > 0, y < 7)))

    @pl.when(jnp.logical_and(far, lower))
    def _():
        pl.semaphore_wait(ready, 1)

        @pl.when(held_up)
        def _():
            a_sends[0].wait_recv()
            a_sends[1].wait_recv()

        b_places.start()
        start(b_sends)

    @pl.when(jnp.logical_or(aside, jnp.logical_and(wrap, jnp.logical_not(early))))
    def _():
        pl.semaphore_wait(ready_last, 1)

    ah, al, bh, bl = (tiles.at[i] for i in range(4))

    def turn(i, carry):
        passing_now = (i == 0) != late

        @pl.when(jnp.logical_and(inner, passing_now))
        def _():
            pass_on()

        @pl.when(jnp.logical_not(passing_now))
        def _():
            for copy in local:
                copy.wait()
            densify(a_own, where.at[0], ah, al)
            densify(b_own, where.at[1], bh, bl)
            for c in range(TB):
                cols = pl.ds(c * BLK, BLK)
                out[:, cols] = three_dots(ah[...], al[...], bh[:, cols], bl[:, cols])

        return carry

    lax.fori_loop(0, 2, turn, 0)

    a_places.wait_recv()

    @pl.when(jnp.logical_not(held_up))
    def _():
        a_sends[0].wait_recv()
        a_sends[1].wait_recv()

    a_sends[2].wait_recv()
    densify(a_in, where.at[2], ah, al)
    b_places.wait_recv()
    positions = where[3]
    for s in range(SLOTS):
        row = positions[:, s : s + 1] // TB
        picked = [jnp.where(row == 0, t[:, :BLK], jnp.where(row == 1, t[:, BLK:], 0)) for t in (ah[...], al[...])]
        b_sends[s].wait_recv()
        term = three_dots(*picked, *halves(b_in[s]))
        for c in range(TB):
            here = jnp.logical_and(positions[:, s : s + 1] % TB == c, row < TB).astype(jnp.float32)
            out[:, pl.ds(c * BLK, BLK)] += here * term

    for copy in [a_places, b_places] + a_sends + b_sends:
        copy.wait_send()

    @pl.when(jnp.logical_or(inner, jnp.logical_and(outer, early)))
    def _():
        for copy in forward:
            copy.wait_send()

    @pl.when(jnp.logical_and(outer, early))
    def _():
        pass_places.wait_send()


def body(a_blocks, a_positions, b_blocks, b_positions):
    held = pltpu.VMEM((SLOTS, BLK, BLK), jnp.float32)
    inputs = (a_blocks[0, 0], a_positions[0], b_blocks[0, 0], b_positions[0])
    return pl.pallas_call(
        kernel,
        out_shape=jax.ShapeDtypeStruct((SIDE, SIDE), jnp.float32),
        in_specs=[pl.BlockSpec(memory_space=pltpu.HBM)] * 4,
        out_specs=pl.BlockSpec(memory_space=pltpu.VMEM),
        scratch_shapes=[
            held,
            held,
            held,
            held,
            pltpu.VMEM((BLK, BLK), jnp.float32),
            pltpu.VMEM((5, 1, SLOTS), jnp.int32),
            pltpu.VMEM((4, SIDE, SIDE), jnp.bfloat16),
            pltpu.SemaphoreType.DMA((4,)),
            pltpu.SemaphoreType.DMA((2, SLOTS + 1)),
            pltpu.SemaphoreType.DMA((2, SLOTS + 1)),
            pltpu.SemaphoreType.DMA((3, PARTS)),
            pltpu.SemaphoreType.REGULAR,
            pltpu.SemaphoreType.REGULAR,
            pltpu.SemaphoreType.REGULAR,
            pltpu.SemaphoreType.REGULAR,
        ],
        compiler_params=pltpu.CompilerParams(
            collective_id=0, has_side_effects=True, vmem_limit_bytes=40 * 1024 * 1024
        ),
    )(*(pltpu.with_memory_space_constraint(v, pltpu.HBM) for v in inputs))


def solution(mesh):
    placed = (
        P("row", "col", None, None, None),
        P("row", "col", None),
        P("row", "col", None, None, None),
        P("row", "col", None),
    )
    return jax.shard_map(body, mesh=mesh, in_specs=placed, out_specs=P("row", "col"), check_vma=False)
```

```python
import jax
import jax.numpy as jnp
from jax import lax
from jax.experimental import pallas as pl
from jax.experimental.pallas import tpu as pltpu
from jax.sharding import PartitionSpec as P

BLK = 256
TB = 2
SLOTS = 3
SIDE = BLK * TB
PARTS = 2
MESH = pl.DeviceIdType.MESH


def place():
    r, c = lax.axis_index("row"), lax.axis_index("col")
    return r // 4, c % 8, (r // 2) % 2 * 4 + c // 8, r % 2


def device(x, y, z, core):
    return (x * 4 + z // 4 * 2 + core, z % 4 * 8 + y)


def along(rows, cols):
    r, c = lax.axis_index("row"), lax.axis_index("col")
    return ((r + rows) % 32, (c + cols) % 32)


def signal(sem, target):
    pl.semaphore_signal(sem, inc=1, device_id=target, device_id_type=MESH)


def start(copies):
    for copy in copies:
        copy.start()


def halves(block):
    top = block.astype(jnp.bfloat16)
    return top, (block - top.astype(jnp.float32)).astype(jnp.bfloat16)


def densify(slots, where, high, low):
    positions = where[...]
    for p in range(TB * TB):
        r, k = p // TB, p % TB
        chosen = [(positions[:, s : s + 1] == p).astype(jnp.float32) for s in range(SLOTS)]
        block = chosen[0] * slots[0] + chosen[1] * slots[1] + chosen[2] * slots[2]
        spot = (pl.ds(r * BLK, BLK), pl.ds(k * BLK, BLK))
        high[spot], low[spot] = halves(block)


def three_dots(lh, ll, rh, rl):
    def dot(u, v):
        return jnp.dot(u, v, preferred_element_type=jnp.float32)

    return dot(lh, rh) + dot(lh, rl) + dot(ll, rh)


def kernel(
    a, a_pos, b, b_pos, out, a_own, b_own, a_in, b_in, passing, where, tiles, load, send, recv, relay, ready, ready_wrap, ready_last, ready_over, ready_next
):
    x, y, z, core = place()
    lo = z % 4
    far = core == 0
    upper = z >= 4
    barrier = pltpu.get_barrier_semaphore()

    local = [
        pltpu.make_async_copy(a, a_own, load.at[0]),
        pltpu.make_async_copy(b, b_own, load.at[1]),
        pltpu.make_async_copy(a_pos, where.at[0], load.at[2]),
        pltpu.make_async_copy(b_pos, where.at[1], load.at[3]),
    ]
    start(local)

    wrap = y == 0
    detour = jnp.where(far, 1, 2)
    aside = y == detour
    outer = y == 7
    lower = jnp.logical_not(upper)
    near = jnp.logical_not(far)
    early, late = lo == 0, lo == 3
    first = z == 0
    told = jnp.logical_and(wrap, first)
    corner = jnp.logical_and(jnp.logical_and(wrap, far), x == 0)
    zero, spared = jnp.logical_and(corner, first), jnp.logical_and(corner, z == 1)
    to_zero = jnp.logical_and(jnp.logical_and(wrap, near), jnp.logical_and(z == 4, x == 7))
    inner = jnp.logical_and(jnp.logical_or(wrap, aside), jnp.logical_not(zero))
    after_zero = jnp.logical_and(jnp.logical_and(inner, far), jnp.logical_and(z == 3, x == 0))
    indirect = jnp.logical_or(early, upper)
    direct = jnp.logical_not(indirect)
    from_zero = jnp.logical_and(jnp.logical_and(first, far), x == 0)
    handing = jnp.logical_and(jnp.logical_and(outer, indirect), jnp.logical_not(from_zero))
    end_of_zero = jnp.logical_and(jnp.logical_and(outer, far), jnp.logical_and(z == 3, x == 0))
    z_to = jnp.where(early, z + 3, z - 1)
    z_from = jnp.where(late, z - 3, z + 1)
    wrap_to = [device(x, 7, z, core), device(x, 0, z_to, core), device(x, detour, z_to, core)]
    wrap_from = device(x, 0, z_from, core)
    last = device(x, 7, z, core)
    last_to, last_from = device(x, 7, z_to, core), device(x, 7, z_from, core)
    a_to, a_from = along(0, -1), along(0, 1)
    b_to, b_from = along(-1, 0), along(1, 0)

    def remote(src, dst, ss, rs, target):
        return pltpu.make_async_remote_copy(
            src_ref=src, dst_ref=dst, send_sem=ss, recv_sem=rs, device_id=target, device_id_type=MESH
        )

    def to_slot(src, which, slot, target):
        dst = (a_in, b_in)[which].at[slot]
        return remote(src, dst, send.at[which, slot], recv.at[which, slot], target)

    a_places = remote(a_pos, where.at[2], send.at[0, SLOTS], recv.at[0, SLOTS], a_to)
    b_places = remote(b_pos, where.at[3], send.at[1, SLOTS], recv.at[1, SLOTS], b_to)
    a_sends = [to_slot(a.at[s], 0, s, a_to) for s in range(SLOTS)]
    b_sends = [to_slot(b.at[s], 1, s, b_to) for s in range(SLOTS)]

    rows = [pl.ds(i * BLK // PARTS, BLK // PARTS) for i in range(PARTS)]
    step_places = remote(a_pos, where.at[4], send.at[0, SLOTS], relay.at[2, 0], wrap_to[0])
    step = [
        [remote(a.at[s, part], passing.at[part], send.at[0, s], relay.at[0, i], wrap_to[s]) for i, part in enumerate(rows)]
        for s in range(SLOTS)
    ]
    slot = jnp.where(outer, 0, jnp.where(wrap, 1, 2))
    target = [jnp.where(outer, u, v) for u, v in zip(last_to, last)]
    pass_places = remote(where.at[4], where.at[2], relay.at[2, 1], recv.at[0, SLOTS], tuple(target))
    forward = [
        remote(passing.at[part], a_in.at[slot, part], relay.at[1, i], recv.at[0, slot], tuple(target))
        for i, part in enumerate(rows)
    ]

    @pl.when(y < 4)
    def _():
        signal(barrier, a_from)

    @pl.when(y > 4)
    def _():
        signal(barrier, a_to)

    @pl.when(jnp.logical_and(inner, jnp.logical_or(jnp.logical_not(late), after_zero)))
    def _():
        signal(barrier, wrap_from)

    @pl.when(jnp.logical_and(wrap, jnp.logical_and(early, jnp.logical_not(zero))))
    def _():
        signal(barrier, wrap_to[1])
        signal(barrier, wrap_to[2])

    @pl.when(jnp.logical_and(wrap, direct))
    def _():
        signal(barrier, last_to)

    @pl.when(jnp.logical_and(outer, jnp.logical_and(upper, jnp.logical_not(late))))
    def _():
        signal(barrier, last_from)

    @pl.when(jnp.logical_and(handing, early))
    def _():
        signal(barrier, last_to)

    @pl.when(end_of_zero)
    def _():
        signal(barrier, wrap_from)

    @pl.when(jnp.logical_and(inner, jnp.logical_not(told)))
    def _():
        signal(barrier, last)

    @pl.when(jnp.logical_and(outer, first))
    def _():
        signal(barrier, device(x, 0, z, core))

    @pl.when(jnp.logical_and(jnp.logical_or(near, lower), jnp.logical_not(zero)))
    def _():
        signal(barrier, b_to)

    @pl.when(jnp.logical_and(near, jnp.logical_or(lower, to_zero)))
    def _():
        signal(barrier, b_from)

    def count(condition, number=1):
        return jnp.where(condition, number, 0)

    replying = jnp.logical_and(y >= 4, y < 7)
    need = count(jnp.logical_and(y > 0, y < 5)) + count(replying) + count(jnp.logical_and(wrap, jnp.logical_not(early)), 2 - count(spared))
    need += count(far) + count(upper) - count(to_zero) + count(zero, 4) + count(told) - count(after_zero)
    need += count(outer, 2 - count(first) + count(z < 3) + count(late) + count(z > 4)) - count(end_of_zero)
    need += count(jnp.logical_and(inner, late))

    @pl.when(need > 0)
    def _():
        pl.semaphore_wait(barrier, need)

    @pl.when(jnp.logical_and(jnp.logical_or(far, upper), jnp.logical_not(to_zero)))
    def _():
        signal(ready, b_from)

    @pl.when(jnp.logical_and(far, jnp.logical_or(upper, zero)))
    def _():
        b_places.start()
        start(b_sends)

    @pl.when(jnp.logical_and(wrap, jnp.logical_and(late, jnp.logical_not(after_zero))))
    def _():
        signal(ready_wrap, wrap_from)

    @pl.when(jnp.logical_and(aside, jnp.logical_and(late, jnp.logical_not(after_zero))))
    def _():
        signal(ready_over, wrap_from)

    @pl.when(outer)
    def _():
        @pl.when(z > 0)
        def _():
            signal(ready_last, device(x, 0, z, core))

        signal(ready_last, device(x, detour, z, core))

        @pl.when(jnp.logical_and(late, jnp.logical_not(end_of_zero)))
        def _():
            signal(ready_wrap, last_from)

        @pl.when(z < 3)
        def _():
            signal(ready_over, wrap_from)

    @pl.when(replying)
    def _():
        signal(ready_next, a_from)

    @pl.when(y > 4)
    def _():
        pl.semaphore_wait(ready_next, 1)

    @pl.when(y > 0)
    def _():
        a_places.start()
        start(a_sends)

    def send_near():
        pl.semaphore_wait(ready, 1)
        b_places.start()
        start(b_sends)

    @pl.when(jnp.logical_and(wrap, jnp.logical_not(early)))
    def _():
        @pl.when(jnp.logical_not(spared))
        def _():
            start(step[1])

        start(step[2])

        @pl.when(upper)
        def _():
            pl.semaphore_wait(ready_last, 1)
            step_places.start()
            start(step[0])

        @pl.when(lower)
        def _():
            pl.semaphore_wait(ready_over, 1)
            a_places.start()
            a_sends[0].start()

        @pl.when(spared)
        def _():
            a_sends[1].start()

    @pl.when(jnp.logical_and(wrap, early))
    def _():
        @pl.when(z > 0)
        def _():
            pl.semaphore_wait(ready_last, 1)

        @pl.when(zero)
        def _():
            a_places.start()
            a_sends[0].start()

        @pl.when(jnp.logical_not(zero))
        def _():
            step_places.start()
            start(step[0])
            pl.semaphore_wait(ready_wrap, 1)

        start(step[1])

        @pl.when(jnp.logical_not(zero))
        def _():
            pl.semaphore_wait(ready_over, 1)

        start(step[2])

    @pl.when(near)
    def _():
        send_near()

    def pass_on():
        for one, other in zip(step[0], forward):
            one.wait_recv()
            other.start()

    def hand_on():
        @pl.when(early)
        def _():
            pl.semaphore_wait(ready_wrap, 1)

        step_places.wait_recv()
        pass_places.start()
        pass_on()

    @pl.when(handing)
    def _():
        hand_on()

    held_up = jnp.logical_and(jnp.logical_and(far, lower), jnp.logical_and(z >= 2, y < 7))

    @pl.when(jnp.logical_and(jnp.logical_and(far, lower), jnp.logical_not(zero)))
    def _():
        pl.semaphore_wait(ready, 1)

        @pl.when(held_up)
        def _():
            a_sends[0].wait_recv()
            a_sends[1].wait_recv()

        b_places.start()
        start(b_sends)

    @pl.when(jnp.logical_or(aside, jnp.logical_and(wrap, direct)))
    def _():
        pl.semaphore_wait(ready_last, 1)

    ah, al, bh, bl = (tiles.at[i] for i in range(4))

    def turn(i, carry):
        passing_now = (i == 0) != jnp.logical_or(late, upper)

        @pl.when(jnp.logical_and(inner, passing_now))
        def _():
            pass_on()

        @pl.when(jnp.logical_not(passing_now))
        def _():
            for copy in local:
                copy.wait()
            densify(a_own, where.at[0], ah, al)
            densify(b_own, where.at[1], bh, bl)
            for c in range(TB):
                cols = pl.ds(c * BLK, BLK)
                out[:, cols] = three_dots(ah[...], al[...], bh[:, cols], bl[:, cols])

        return carry

    lax.fori_loop(0, 2, turn, 0)

    a_places.wait_recv()

    @pl.when(jnp.logical_not(held_up))
    def _():
        a_sends[0].wait_recv()
        a_sends[1].wait_recv()

    a_sends[2].wait_recv()
    densify(a_in, where.at[2], ah, al)
    b_places.wait_recv()
    positions = where[3]
    for s in range(SLOTS):
        row = positions[:, s : s + 1] // TB
        picked = [jnp.where(row == 0, t[:, :BLK], jnp.where(row == 1, t[:, BLK:], 0)) for t in (ah[...], al[...])]
        b_sends[s].wait_recv()
        term = three_dots(*picked, *halves(b_in[s]))
        for c in range(TB):
            here = jnp.logical_and(positions[:, s : s + 1] % TB == c, row < TB).astype(jnp.float32)
            out[:, pl.ds(c * BLK, BLK)] += here * term

    for copy in [a_places, b_places] + a_sends + b_sends:
        copy.wait_send()

    @pl.when(jnp.logical_or(inner, handing))
    def _():
        for copy in forward:
            copy.wait_send()

    @pl.when(handing)
    def _():
        pass_places.wait_send()


def body(a_blocks, a_positions, b_blocks, b_positions):
    held = pltpu.VMEM((SLOTS, BLK, BLK), jnp.float32)
    inputs = (a_blocks[0, 0], a_positions[0], b_blocks[0, 0], b_positions[0])
    return pl.pallas_call(
        kernel,
        out_shape=jax.ShapeDtypeStruct((SIDE, SIDE), jnp.float32),
        in_specs=[pl.BlockSpec(memory_space=pltpu.HBM)] * 4,
        out_specs=pl.BlockSpec(memory_space=pltpu.VMEM),
        scratch_shapes=[
            held,
            held,
            held,
            held,
            pltpu.VMEM((BLK, BLK), jnp.float32),
            pltpu.VMEM((5, 1, SLOTS), jnp.int32),
            pltpu.VMEM((4, SIDE, SIDE), jnp.bfloat16),
            pltpu.SemaphoreType.DMA((4,)),
            pltpu.SemaphoreType.DMA((2, SLOTS + 1)),
            pltpu.SemaphoreType.DMA((2, SLOTS + 1)),
            pltpu.SemaphoreType.DMA((3, PARTS)),
            pltpu.SemaphoreType.REGULAR,
            pltpu.SemaphoreType.REGULAR,
            pltpu.SemaphoreType.REGULAR,
            pltpu.SemaphoreType.REGULAR,
            pltpu.SemaphoreType.REGULAR,
        ],
        compiler_params=pltpu.CompilerParams(
            collective_id=0, has_side_effects=True, vmem_limit_bytes=40 * 1024 * 1024
        ),
    )(*(pltpu.with_memory_space_constraint(v, pltpu.HBM) for v in inputs))


def solution(mesh):
    placed = (
        P("row", "col", None, None, None),
        P("row", "col", None),
        P("row", "col", None, None, None),
        P("row", "col", None),
    )
    return jax.shard_map(body, mesh=mesh, in_specs=placed, out_specs=P("row", "col"), check_vma=False)
```

```python
import jax
import jax.numpy as jnp
from jax import lax
from jax.experimental import pallas as pl
from jax.experimental.pallas import tpu as pltpu
from jax.sharding import PartitionSpec as P

BLK = 256
TB = 2
SLOTS = 3
SIDE = BLK * TB
PARTS = 2
MESH = pl.DeviceIdType.MESH


def place():
    r, c = lax.axis_index("row"), lax.axis_index("col")
    return r // 4, c % 8, (r // 2) % 2 * 4 + c // 8, r % 2


def device(x, y, z, core):
    return (x * 4 + z // 4 * 2 + core, z % 4 * 8 + y)


def along(rows, cols):
    r, c = lax.axis_index("row"), lax.axis_index("col")
    return ((r + rows) % 32, (c + cols) % 32)


def signal(sem, target):
    pl.semaphore_signal(sem, inc=1, device_id=target, device_id_type=MESH)


def start(copies):
    for copy in copies:
        copy.start()


def halves(block):
    top = block.astype(jnp.bfloat16)
    return top, (block - top.astype(jnp.float32)).astype(jnp.bfloat16)


def densify(slots, where, high, low):
    positions = where[...]
    for p in range(TB * TB):
        r, k = p // TB, p % TB
        chosen = [(positions[:, s : s + 1] == p).astype(jnp.float32) for s in range(SLOTS)]
        block = chosen[0] * slots[0] + chosen[1] * slots[1] + chosen[2] * slots[2]
        spot = (pl.ds(r * BLK, BLK), pl.ds(k * BLK, BLK))
        high[spot], low[spot] = halves(block)


def three_dots(lh, ll, rh, rl):
    def dot(u, v):
        return jnp.dot(u, v, preferred_element_type=jnp.float32)

    return dot(lh, rh) + dot(lh, rl) + dot(ll, rh)


def kernel(
    a, a_pos, b, b_pos, out, a_own, b_own, a_in, b_in, passing, where, tiles, load, send, recv, relay, ready, ready_wrap, ready_last, ready_over, ready_next
):
    x, y, z, core = place()
    lo = z % 4
    far = core == 0
    upper = z >= 4
    barrier = pltpu.get_barrier_semaphore()

    local = [
        pltpu.make_async_copy(a, a_own, load.at[0]),
        pltpu.make_async_copy(b, b_own, load.at[1]),
        pltpu.make_async_copy(a_pos, where.at[0], load.at[2]),
        pltpu.make_async_copy(b_pos, where.at[1], load.at[3]),
    ]
    start(local)

    wrap = y == 0
    detour = jnp.where(far, 1, 2)
    aside = y == detour
    outer = y == 7
    lower = jnp.logical_not(upper)
    near = jnp.logical_not(far)
    early, late = lo == 0, lo == 3
    first = z == 0
    told = jnp.logical_and(wrap, first)
    corner = jnp.logical_and(jnp.logical_and(wrap, far), x == 0)
    zero, spared = jnp.logical_and(corner, first), jnp.logical_and(corner, z == 1)
    to_zero = jnp.logical_and(jnp.logical_and(wrap, near), jnp.logical_and(z == 4, x == 7))
    inner = jnp.logical_and(jnp.logical_or(wrap, aside), jnp.logical_not(zero))
    after_zero = jnp.logical_and(jnp.logical_and(inner, far), jnp.logical_and(z == 3, x == 0))
    indirect = jnp.logical_or(early, upper)
    direct = jnp.logical_not(indirect)
    from_zero = jnp.logical_and(jnp.logical_and(first, far), x == 0)
    handing = jnp.logical_and(jnp.logical_and(outer, indirect), jnp.logical_not(from_zero))
    end_of_zero = jnp.logical_and(jnp.logical_and(outer, far), jnp.logical_and(z == 3, x == 0))
    z_to = jnp.where(early, z + 3, z - 1)
    z_from = jnp.where(late, z - 3, z + 1)
    wrap_to = [device(x, 7, z, core), device(x, 0, z_to, core), device(x, detour, z_to, core)]
    wrap_from = device(x, 0, z_from, core)
    last = device(x, 7, z, core)
    last_to, last_from = device(x, 7, z_to, core), device(x, 7, z_from, core)
    a_to, a_from = along(0, -1), along(0, 1)
    b_to, b_from = along(-1, 0), along(1, 0)

    def remote(src, dst, ss, rs, target):
        return pltpu.make_async_remote_copy(
            src_ref=src, dst_ref=dst, send_sem=ss, recv_sem=rs, device_id=target, device_id_type=MESH
        )

    def to_slot(src, which, slot, target):
        dst = (a_in, b_in)[which].at[slot]
        return remote(src, dst, send.at[which, slot], recv.at[which, slot], target)

    a_places = remote(a_pos, where.at[2], send.at[0, SLOTS], recv.at[0, SLOTS], a_to)
    b_places = remote(b_pos, where.at[3], send.at[1, SLOTS], recv.at[1, SLOTS], b_to)
    a_sends = [to_slot(a.at[s], 0, s, a_to) for s in range(SLOTS)]
    b_sends = [to_slot(b.at[s], 1, s, b_to) for s in range(SLOTS)]

    rows = [pl.ds(i * BLK // PARTS, BLK // PARTS) for i in range(PARTS)]
    step_places = remote(a_pos, where.at[4], send.at[0, SLOTS], relay.at[2, 0], wrap_to[0])
    step = [
        [remote(a.at[s, part], passing.at[part], send.at[0, s], relay.at[0, i], wrap_to[s]) for i, part in enumerate(rows)]
        for s in range(SLOTS)
    ]
    slot = jnp.where(outer, 0, jnp.where(wrap, 1, 2))
    target = [jnp.where(outer, u, v) for u, v in zip(last_to, last)]
    pass_places = remote(where.at[4], where.at[2], relay.at[2, 1], recv.at[0, SLOTS], tuple(target))
    forward = [
        remote(passing.at[part], a_in.at[slot, part], relay.at[1, i], recv.at[0, slot], tuple(target))
        for i, part in enumerate(rows)
    ]

    @pl.when(y < 4)
    def _():
        signal(barrier, a_from)

    @pl.when(y > 4)
    def _():
        signal(barrier, a_to)

    @pl.when(jnp.logical_and(inner, jnp.logical_or(jnp.logical_not(late), after_zero)))
    def _():
        signal(barrier, wrap_from)

    @pl.when(jnp.logical_and(wrap, jnp.logical_and(early, jnp.logical_not(zero))))
    def _():
        signal(barrier, wrap_to[1])
        signal(barrier, wrap_to[2])

    @pl.when(jnp.logical_and(wrap, direct))
    def _():
        signal(barrier, last_to)

    @pl.when(jnp.logical_and(outer, jnp.logical_and(upper, jnp.logical_not(late))))
    def _():
        signal(barrier, last_from)

    @pl.when(jnp.logical_and(handing, early))
    def _():
        signal(barrier, last_to)

    @pl.when(end_of_zero)
    def _():
        signal(barrier, wrap_from)

    @pl.when(jnp.logical_and(inner, jnp.logical_not(told)))
    def _():
        signal(barrier, last)

    @pl.when(jnp.logical_and(outer, first))
    def _():
        signal(barrier, device(x, 0, z, core))

    @pl.when(jnp.logical_and(jnp.logical_or(near, lower), jnp.logical_not(zero)))
    def _():
        signal(barrier, b_to)

    @pl.when(jnp.logical_and(near, jnp.logical_or(lower, to_zero)))
    def _():
        signal(barrier, b_from)

    def count(condition, number=1):
        return jnp.where(condition, number, 0)

    replying = jnp.logical_and(y >= 4, y < 7)
    need = count(jnp.logical_and(y > 0, y < 5)) + count(replying) + count(jnp.logical_and(wrap, jnp.logical_not(early)), 2 - count(spared))
    need += count(far) + count(upper) - count(to_zero) + count(zero, 4) + count(told) - count(after_zero)
    need += count(outer, 2 - count(first) + count(z < 3) + count(late) + count(z > 4)) - count(end_of_zero)
    need += count(jnp.logical_and(inner, late))

    @pl.when(need > 0)
    def _():
        pl.semaphore_wait(barrier, need)

    @pl.when(jnp.logical_and(jnp.logical_or(far, upper), jnp.logical_not(to_zero)))
    def _():
        signal(ready, b_from)

    @pl.when(jnp.logical_and(far, jnp.logical_or(upper, zero)))
    def _():
        b_places.start()
        start(b_sends)

    @pl.when(jnp.logical_and(wrap, jnp.logical_and(late, jnp.logical_not(after_zero))))
    def _():
        signal(ready_wrap, wrap_from)

    @pl.when(jnp.logical_and(aside, jnp.logical_and(late, jnp.logical_not(after_zero))))
    def _():
        signal(ready_over, wrap_from)

    @pl.when(outer)
    def _():
        @pl.when(z > 0)
        def _():
            signal(ready_last, device(x, 0, z, core))

        signal(ready_last, device(x, detour, z, core))

        @pl.when(jnp.logical_and(late, jnp.logical_not(end_of_zero)))
        def _():
            signal(ready_wrap, last_from)

        @pl.when(z < 3)
        def _():
            signal(ready_over, wrap_from)

    @pl.when(replying)
    def _():
        signal(ready_next, a_from)

    @pl.when(y > 4)
    def _():
        pl.semaphore_wait(ready_next, 1)

    @pl.when(y > 0)
    def _():
        a_places.start()
        start(a_sends)

    def send_near():
        pl.semaphore_wait(ready, 1)
        b_places.start()
        start(b_sends)

    @pl.when(jnp.logical_and(wrap, jnp.logical_not(early)))
    def _():
        @pl.when(jnp.logical_not(spared))
        def _():
            start(step[1])

        start(step[2])

        @pl.when(upper)
        def _():
            pl.semaphore_wait(ready_last, 1)
            step_places.start()
            start(step[0])

        @pl.when(lower)
        def _():
            pl.semaphore_wait(ready_over, 1)
            a_places.start()
            a_sends[0].start()

        @pl.when(spared)
        def _():
            a_sends[1].start()

    @pl.when(jnp.logical_and(near, upper))
    def _():
        send_near()

    waiting = jnp.logical_and(wrap, z == 4)

    @pl.when(waiting)
    def _():
        for copy in a_sends[:2]:
            copy.wait_recv()

    @pl.when(jnp.logical_and(wrap, early))
    def _():
        @pl.when(z > 0)
        def _():
            pl.semaphore_wait(ready_last, 1)

        @pl.when(zero)
        def _():
            a_places.start()
            a_sends[0].start()

        @pl.when(jnp.logical_not(zero))
        def _():
            step_places.start()
            start(step[0])
            pl.semaphore_wait(ready_wrap, 1)

        start(step[1])

        @pl.when(jnp.logical_not(zero))
        def _():
            pl.semaphore_wait(ready_over, 1)

        start(step[2])

    @pl.when(jnp.logical_and(near, lower))
    def _():
        send_near()

    def pass_on():
        for one, other in zip(step[0], forward):
            one.wait_recv()
            other.start()

    def hand_on():
        @pl.when(early)
        def _():
            pl.semaphore_wait(ready_wrap, 1)

        step_places.wait_recv()
        pass_places.start()
        pass_on()

    @pl.when(jnp.logical_and(handing, z != 4))
    def _():
        hand_on()

    held_up = jnp.logical_and(jnp.logical_and(far, lower), jnp.logical_and(z >= 2, y < 7))
    held_last = jnp.logical_and(jnp.logical_and(far, lower), jnp.logical_and(z >= 2, outer))

    @pl.when(jnp.logical_and(jnp.logical_and(far, lower), jnp.logical_not(zero)))
    def _():
        pl.semaphore_wait(ready, 1)

        @pl.when(held_up)
        def _():
            a_sends[0].wait_recv()
            a_sends[1].wait_recv()

        @pl.when(held_last)
        def _():
            for copy in a_sends:
                copy.wait_send()

        b_places.start()
        start(b_sends)

    @pl.when(jnp.logical_or(aside, jnp.logical_and(wrap, direct)))
    def _():
        pl.semaphore_wait(ready_last, 1)

    ah, al, bh, bl = (tiles.at[i] for i in range(4))

    def turn(i, carry):
        passing_now = (i == 0) != jnp.logical_or(late, upper)

        @pl.when(jnp.logical_and(inner, passing_now))
        def _():
            pass_on()

        @pl.when(jnp.logical_and(jnp.logical_and(handing, z == 4), passing_now))
        def _():
            hand_on()

        @pl.when(jnp.logical_not(passing_now))
        def _():
            for copy in local:
                copy.wait()
            densify(a_own, where.at[0], ah, al)
            densify(b_own, where.at[1], bh, bl)
            for c in range(TB):
                cols = pl.ds(c * BLK, BLK)
                out[:, cols] = three_dots(ah[...], al[...], bh[:, cols], bl[:, cols])

        return carry

    lax.fori_loop(0, 2, turn, 0)

    a_last = jnp.logical_and(outer, jnp.logical_or(upper, jnp.logical_and(late, far)))

    @pl.when(a_last)
    def _():
        b_places.wait_recv()
        for copy in b_sends:
            copy.wait_recv()
        densify(b_in, where.at[3], bh, bl)
        a_places.wait_recv()
        positions = where[2]
        for s in range(SLOTS):
            row = positions[:, s : s + 1] // TB
            col = positions[:, s : s + 1] % TB
            picked = [jnp.where(col == 0, t[:BLK], t[BLK:]) for t in (bh[...], bl[...])]
            a_sends[s].wait_recv()
            term = three_dots(*halves(a_in[s]), *picked)
            for r in range(TB):
                out[pl.ds(r * BLK, BLK), :] += (row == r).astype(jnp.float32) * term

    @pl.when(jnp.logical_not(a_last))
    def _():
        a_places.wait_recv()

        @pl.when(jnp.logical_not(jnp.logical_or(held_up, waiting)))
        def _():
            a_sends[0].wait_recv()
            a_sends[1].wait_recv()

        a_sends[2].wait_recv()
        densify(a_in, where.at[2], ah, al)
        b_places.wait_recv()
        positions = where[3]
        for s in range(SLOTS):
            row = positions[:, s : s + 1] // TB
            picked = [jnp.where(row == 0, t[:, :BLK], jnp.where(row == 1, t[:, BLK:], 0)) for t in (ah[...], al[...])]
            b_sends[s].wait_recv()
            term = three_dots(*picked, *halves(b_in[s]))
            for c in range(TB):
                here = jnp.logical_and(positions[:, s : s + 1] % TB == c, row < TB).astype(jnp.float32)
                out[:, pl.ds(c * BLK, BLK)] += here * term

    @pl.when(jnp.logical_not(held_last))
    def _():
        for copy in a_sends:
            copy.wait_send()

    for copy in [a_places, b_places] + b_sends:
        copy.wait_send()

    @pl.when(jnp.logical_or(inner, handing))
    def _():
        for copy in forward:
            copy.wait_send()

    @pl.when(handing)
    def _():
        pass_places.wait_send()


def body(a_blocks, a_positions, b_blocks, b_positions):
    held = pltpu.VMEM((SLOTS, BLK, BLK), jnp.float32)
    inputs = (a_blocks[0, 0], a_positions[0], b_blocks[0, 0], b_positions[0])
    return pl.pallas_call(
        kernel,
        out_shape=jax.ShapeDtypeStruct((SIDE, SIDE), jnp.float32),
        in_specs=[pl.BlockSpec(memory_space=pltpu.HBM)] * 4,
        out_specs=pl.BlockSpec(memory_space=pltpu.VMEM),
        scratch_shapes=[
            held,
            held,
            held,
            held,
            pltpu.VMEM((BLK, BLK), jnp.float32),
            pltpu.VMEM((5, 1, SLOTS), jnp.int32),
            pltpu.VMEM((4, SIDE, SIDE), jnp.bfloat16),
            pltpu.SemaphoreType.DMA((4,)),
            pltpu.SemaphoreType.DMA((2, SLOTS + 1)),
            pltpu.SemaphoreType.DMA((2, SLOTS + 1)),
            pltpu.SemaphoreType.DMA((3, PARTS)),
            pltpu.SemaphoreType.REGULAR,
            pltpu.SemaphoreType.REGULAR,
            pltpu.SemaphoreType.REGULAR,
            pltpu.SemaphoreType.REGULAR,
            pltpu.SemaphoreType.REGULAR,
        ],
        compiler_params=pltpu.CompilerParams(
            collective_id=0, has_side_effects=True, vmem_limit_bytes=40 * 1024 * 1024
        ),
    )(*(pltpu.with_memory_space_constraint(v, pltpu.HBM) for v in inputs))


def solution(mesh):
    placed = (
        P("row", "col", None, None, None),
        P("row", "col", None),
        P("row", "col", None, None, None),
        P("row", "col", None),
    )
    return jax.shard_map(body, mesh=mesh, in_specs=placed, out_specs=P("row", "col"), check_vma=False)
```

```python
import jax
import jax.numpy as jnp
from jax import lax
from jax.experimental import pallas as pl
from jax.experimental.pallas import tpu as pltpu
from jax.sharding import PartitionSpec as P

BLK = 256
TB = 2
SLOTS = 3
SIDE = BLK * TB
PARTS = 2
MESH = pl.DeviceIdType.MESH


def place():
    r, c = lax.axis_index("row"), lax.axis_index("col")
    return r // 4, c % 8, (r // 2) % 2 * 4 + c // 8, r % 2


def device(x, y, z, core):
    return (x * 4 + z // 4 * 2 + core, z % 4 * 8 + y)


def along(rows, cols):
    r, c = lax.axis_index("row"), lax.axis_index("col")
    return ((r + rows) % 32, (c + cols) % 32)


def signal(sem, target):
    pl.semaphore_signal(sem, inc=1, device_id=target, device_id_type=MESH)


def start(copies):
    for copy in copies:
        copy.start()


def halves(block):
    top = block.astype(jnp.bfloat16)
    return top, (block - top.astype(jnp.float32)).astype(jnp.bfloat16)


def densify(slots, where, high, low):
    positions = where[...]
    for p in range(TB * TB):
        r, k = p // TB, p % TB
        chosen = [(positions[:, s : s + 1] == p).astype(jnp.float32) for s in range(SLOTS)]
        block = chosen[0] * slots[0] + chosen[1] * slots[1] + chosen[2] * slots[2]
        spot = (pl.ds(r * BLK, BLK), pl.ds(k * BLK, BLK))
        high[spot], low[spot] = halves(block)


def three_dots(lh, ll, rh, rl):
    def dot(u, v):
        return jnp.dot(u, v, preferred_element_type=jnp.float32)

    return dot(lh, rh) + dot(lh, rl) + dot(ll, rh)


def kernel(
    a, a_pos, b, b_pos, out, a_own, b_own, a_in, b_in, passing, where, tiles, load, send, recv, relay, ready, ready_wrap, ready_last, ready_over, ready_next
):
    x, y, z, core = place()
    lo = z % 4
    far = core == 0
    upper = z >= 4
    barrier = pltpu.get_barrier_semaphore()

    local = [
        pltpu.make_async_copy(a, a_own, load.at[0]),
        pltpu.make_async_copy(b, b_own, load.at[1]),
        pltpu.make_async_copy(a_pos, where.at[0], load.at[2]),
        pltpu.make_async_copy(b_pos, where.at[1], load.at[3]),
    ]
    start(local)

    wrap = y == 0
    detour = jnp.where(far, 1, 2)
    aside = y == detour
    outer = y == 7
    lower = jnp.logical_not(upper)
    near = jnp.logical_not(far)
    early, late = lo == 0, lo == 3
    first = z == 0
    told = jnp.logical_and(wrap, first)
    corner = jnp.logical_and(jnp.logical_and(wrap, far), x == 0)
    zero, spared = jnp.logical_and(corner, first), jnp.logical_and(corner, z == 1)
    to_zero = jnp.logical_and(jnp.logical_and(wrap, near), jnp.logical_and(z == 4, x == 7))
    inner = jnp.logical_and(jnp.logical_or(wrap, aside), jnp.logical_not(zero))
    after_zero = jnp.logical_and(jnp.logical_and(inner, far), jnp.logical_and(z == 3, x == 0))
    indirect = jnp.logical_or(early, upper)
    direct = jnp.logical_not(indirect)
    from_zero = jnp.logical_and(jnp.logical_and(first, far), x == 0)
    handing = jnp.logical_and(jnp.logical_and(outer, indirect), jnp.logical_not(from_zero))
    end_of_zero = jnp.logical_and(jnp.logical_and(outer, far), jnp.logical_and(z == 3, x == 0))
    z_to = jnp.where(early, z + 3, z - 1)
    z_from = jnp.where(late, z - 3, z + 1)
    wrap_to = [device(x, 7, z, core), device(x, 0, z_to, core), device(x, detour, z_to, core)]
    wrap_from = device(x, 0, z_from, core)
    last = device(x, 7, z, core)
    last_to, last_from = device(x, 7, z_to, core), device(x, 7, z_from, core)
    a_to, a_from = along(0, -1), along(0, 1)
    b_to, b_from = along(-1, 0), along(1, 0)

    def remote(src, dst, ss, rs, target):
        return pltpu.make_async_remote_copy(
            src_ref=src, dst_ref=dst, send_sem=ss, recv_sem=rs, device_id=target, device_id_type=MESH
        )

    def to_slot(src, which, slot, target):
        dst = (a_in, b_in)[which].at[slot]
        return remote(src, dst, send.at[which, slot], recv.at[which, slot], target)

    a_places = remote(a_pos, where.at[2], send.at[0, SLOTS], recv.at[0, SLOTS], a_to)
    b_places = remote(b_pos, where.at[3], send.at[1, SLOTS], recv.at[1, SLOTS], b_to)
    a_sends = [to_slot(a.at[s], 0, s, a_to) for s in range(SLOTS)]
    b_sends = [to_slot(b.at[s], 1, s, b_to) for s in range(SLOTS)]

    rows = [pl.ds(i * BLK // PARTS, BLK // PARTS) for i in range(PARTS)]
    step_places = remote(a_pos, where.at[4], send.at[0, SLOTS], relay.at[2, 0], wrap_to[0])
    step = [
        [remote(a.at[s, part], passing.at[part], send.at[0, s], relay.at[0, i], wrap_to[s]) for i, part in enumerate(rows)]
        for s in range(SLOTS)
    ]
    slot = jnp.where(outer, 0, jnp.where(wrap, 1, 2))
    target = [jnp.where(outer, u, v) for u, v in zip(last_to, last)]
    pass_places = remote(where.at[4], where.at[2], relay.at[2, 1], recv.at[0, SLOTS], tuple(target))
    forward = [
        remote(passing.at[part], a_in.at[slot, part], relay.at[1, i], recv.at[0, slot], tuple(target))
        for i, part in enumerate(rows)
    ]

    @pl.when(y < 4)
    def _():
        signal(barrier, a_from)

    @pl.when(y > 4)
    def _():
        signal(barrier, a_to)

    @pl.when(jnp.logical_and(inner, jnp.logical_or(jnp.logical_not(late), after_zero)))
    def _():
        signal(barrier, wrap_from)

    @pl.when(jnp.logical_and(wrap, jnp.logical_and(early, jnp.logical_not(zero))))
    def _():
        signal(barrier, wrap_to[1])
        signal(barrier, wrap_to[2])

    @pl.when(jnp.logical_and(wrap, direct))
    def _():
        signal(barrier, last_to)

    @pl.when(jnp.logical_and(outer, jnp.logical_and(upper, jnp.logical_not(late))))
    def _():
        signal(barrier, last_from)

    @pl.when(jnp.logical_and(handing, early))
    def _():
        signal(barrier, last_to)

    @pl.when(end_of_zero)
    def _():
        signal(barrier, wrap_from)

    @pl.when(jnp.logical_and(inner, jnp.logical_not(told)))
    def _():
        signal(barrier, last)

    @pl.when(jnp.logical_and(outer, first))
    def _():
        signal(barrier, device(x, 0, z, core))

    @pl.when(jnp.logical_and(jnp.logical_or(near, lower), jnp.logical_not(zero)))
    def _():
        signal(barrier, b_to)

    @pl.when(jnp.logical_and(near, jnp.logical_or(lower, to_zero)))
    def _():
        signal(barrier, b_from)

    def count(condition, number=1):
        return jnp.where(condition, number, 0)

    replying = jnp.logical_and(y >= 4, y < 7)
    need = count(jnp.logical_and(y > 0, y < 5)) + count(replying) + count(jnp.logical_and(wrap, jnp.logical_not(early)), 2 - count(spared))
    need += count(far) + count(upper) - count(to_zero) + count(zero, 4) + count(told) - count(after_zero)
    need += count(outer, 2 - count(first) + count(z < 3) + count(late) + count(z > 4)) - count(end_of_zero)
    need += count(jnp.logical_and(inner, late))

    @pl.when(need > 0)
    def _():
        pl.semaphore_wait(barrier, need)

    @pl.when(jnp.logical_and(jnp.logical_or(far, upper), jnp.logical_not(to_zero)))
    def _():
        signal(ready, b_from)

    @pl.when(jnp.logical_and(far, jnp.logical_or(upper, zero)))
    def _():
        b_places.start()
        start(b_sends)

    @pl.when(jnp.logical_and(wrap, jnp.logical_and(late, jnp.logical_not(after_zero))))
    def _():
        signal(ready_wrap, wrap_from)

    @pl.when(jnp.logical_and(aside, jnp.logical_and(late, jnp.logical_not(after_zero))))
    def _():
        signal(ready_over, wrap_from)

    @pl.when(outer)
    def _():
        @pl.when(z > 0)
        def _():
            signal(ready_last, device(x, 0, z, core))

        signal(ready_last, device(x, detour, z, core))

        @pl.when(jnp.logical_and(late, jnp.logical_not(end_of_zero)))
        def _():
            signal(ready_wrap, last_from)

        @pl.when(z < 3)
        def _():
            signal(ready_over, wrap_from)

    @pl.when(replying)
    def _():
        signal(ready_next, a_from)

    @pl.when(y > 4)
    def _():
        pl.semaphore_wait(ready_next, 1)

    @pl.when(y > 0)
    def _():
        a_places.start()
        start(a_sends)

    def send_near():
        pl.semaphore_wait(ready, 1)
        b_places.start()
        start(b_sends)

    @pl.when(jnp.logical_and(wrap, jnp.logical_not(early)))
    def _():
        @pl.when(jnp.logical_not(spared))
        def _():
            start(step[1])

        start(step[2])

        @pl.when(upper)
        def _():
            pl.semaphore_wait(ready_last, 1)
            step_places.start()
            start(step[0])

        @pl.when(lower)
        def _():
            pl.semaphore_wait(ready_over, 1)
            a_places.start()
            a_sends[0].start()

        @pl.when(spared)
        def _():
            a_sends[1].start()

    @pl.when(jnp.logical_and(near, upper))
    def _():
        send_near()

    waiting = jnp.logical_and(wrap, z == 4)

    @pl.when(waiting)
    def _():
        for copy in a_sends[:2]:
            copy.wait_recv()

    @pl.when(jnp.logical_and(wrap, early))
    def _():
        @pl.when(z > 0)
        def _():
            pl.semaphore_wait(ready_last, 1)

        @pl.when(zero)
        def _():
            a_places.start()
            a_sends[0].start()

        @pl.when(jnp.logical_not(zero))
        def _():
            step_places.start()
            start(step[0])
            pl.semaphore_wait(ready_wrap, 1)

        start(step[1])

        @pl.when(jnp.logical_not(zero))
        def _():
            pl.semaphore_wait(ready_over, 1)

        start(step[2])

    @pl.when(jnp.logical_and(near, lower))
    def _():
        send_near()

    def pass_on():
        for one, other in zip(step[0], forward):
            one.wait_recv()
            other.start()

    def hand_on():
        @pl.when(early)
        def _():
            pl.semaphore_wait(ready_wrap, 1)

        step_places.wait_recv()
        pass_places.start()
        pass_on()

    @pl.when(jnp.logical_and(handing, z != 4))
    def _():
        hand_on()

    held_up = jnp.logical_and(jnp.logical_and(far, lower), jnp.logical_and(z >= 2, wrap))
    held_last = jnp.logical_and(jnp.logical_and(far, lower), jnp.logical_and(z >= 2, y > 0))

    @pl.when(jnp.logical_and(jnp.logical_and(far, lower), jnp.logical_not(zero)))
    def _():
        pl.semaphore_wait(ready, 1)

        @pl.when(held_up)
        def _():
            a_sends[0].wait_recv()
            a_sends[1].wait_recv()

            @pl.when(late)
            def _():
                a_sends[2].wait_recv()

        @pl.when(held_last)
        def _():
            for copy in a_sends:
                copy.wait_send()

        b_places.start()
        start(b_sends)

    @pl.when(jnp.logical_or(aside, jnp.logical_and(wrap, direct)))
    def _():
        pl.semaphore_wait(ready_last, 1)

    ah, al, bh, bl = (tiles.at[i] for i in range(4))

    def turn(i, carry):
        passing_now = (i == 0) != jnp.logical_or(late, upper)

        @pl.when(jnp.logical_and(inner, passing_now))
        def _():
            pass_on()

        @pl.when(jnp.logical_and(jnp.logical_and(handing, z == 4), passing_now))
        def _():
            hand_on()

        @pl.when(jnp.logical_not(passing_now))
        def _():
            for copy in local:
                copy.wait()
            densify(a_own, where.at[0], ah, al)
            densify(b_own, where.at[1], bh, bl)
            for c in range(TB):
                cols = pl.ds(c * BLK, BLK)
                out[:, cols] = three_dots(ah[...], al[...], bh[:, cols], bl[:, cols])

        return carry

    lax.fori_loop(0, 2, turn, 0)

    a_last = jnp.logical_and(outer, jnp.logical_or(upper, jnp.logical_and(late, far)))

    @pl.when(a_last)
    def _():
        b_places.wait_recv()
        for copy in b_sends:
            copy.wait_recv()
        densify(b_in, where.at[3], bh, bl)
        a_places.wait_recv()
        positions = where[2]
        for s in range(SLOTS):
            row = positions[:, s : s + 1] // TB
            col = positions[:, s : s + 1] % TB
            picked = [jnp.where(col == 0, t[:BLK], t[BLK:]) for t in (bh[...], bl[...])]
            a_sends[s].wait_recv()
            term = three_dots(*halves(a_in[s]), *picked)
            for r in range(TB):
                out[pl.ds(r * BLK, BLK), :] += (row == r).astype(jnp.float32) * term

    @pl.when(jnp.logical_not(a_last))
    def _():
        a_places.wait_recv()

        @pl.when(jnp.logical_not(jnp.logical_or(held_up, waiting)))
        def _():
            a_sends[0].wait_recv()
            a_sends[1].wait_recv()

        @pl.when(jnp.logical_not(jnp.logical_and(held_up, late)))
        def _():
            a_sends[2].wait_recv()

        densify(a_in, where.at[2], ah, al)
        b_places.wait_recv()
        positions = where[3]
        for s in range(SLOTS):
            row = positions[:, s : s + 1] // TB
            picked = [jnp.where(row == 0, t[:, :BLK], jnp.where(row == 1, t[:, BLK:], 0)) for t in (ah[...], al[...])]
            b_sends[s].wait_recv()
            term = three_dots(*picked, *halves(b_in[s]))
            for c in range(TB):
                here = jnp.logical_and(positions[:, s : s + 1] % TB == c, row < TB).astype(jnp.float32)
                out[:, pl.ds(c * BLK, BLK)] += here * term

    @pl.when(jnp.logical_not(held_last))
    def _():
        for copy in a_sends:
            copy.wait_send()

    for copy in [a_places, b_places] + b_sends:
        copy.wait_send()

    @pl.when(jnp.logical_or(inner, handing))
    def _():
        for copy in forward:
            copy.wait_send()

    @pl.when(handing)
    def _():
        pass_places.wait_send()


def body(a_blocks, a_positions, b_blocks, b_positions):
    held = pltpu.VMEM((SLOTS, BLK, BLK), jnp.float32)
    inputs = (a_blocks[0, 0], a_positions[0], b_blocks[0, 0], b_positions[0])
    return pl.pallas_call(
        kernel,
        out_shape=jax.ShapeDtypeStruct((SIDE, SIDE), jnp.float32),
        in_specs=[pl.BlockSpec(memory_space=pltpu.HBM)] * 4,
        out_specs=pl.BlockSpec(memory_space=pltpu.VMEM),
        scratch_shapes=[
            held,
            held,
            held,
            held,
            pltpu.VMEM((BLK, BLK), jnp.float32),
            pltpu.VMEM((5, 1, SLOTS), jnp.int32),
            pltpu.VMEM((4, SIDE, SIDE), jnp.bfloat16),
            pltpu.SemaphoreType.DMA((4,)),
            pltpu.SemaphoreType.DMA((2, SLOTS + 1)),
            pltpu.SemaphoreType.DMA((2, SLOTS + 1)),
            pltpu.SemaphoreType.DMA((3, PARTS)),
            pltpu.SemaphoreType.REGULAR,
            pltpu.SemaphoreType.REGULAR,
            pltpu.SemaphoreType.REGULAR,
            pltpu.SemaphoreType.REGULAR,
            pltpu.SemaphoreType.REGULAR,
        ],
        compiler_params=pltpu.CompilerParams(
            collective_id=0, has_side_effects=True, vmem_limit_bytes=40 * 1024 * 1024
        ),
    )(*(pltpu.with_memory_space_constraint(v, pltpu.HBM) for v in inputs))


def solution(mesh):
    placed = (
        P("row", "col", None, None, None),
        P("row", "col", None),
        P("row", "col", None, None, None),
        P("row", "col", None),
    )
    return jax.shard_map(body, mesh=mesh, in_specs=placed, out_specs=P("row", "col"), check_vma=False)
```

```python
import jax
import jax.numpy as jnp
from jax import lax
from jax.experimental import pallas as pl
from jax.experimental.pallas import tpu as pltpu
from jax.sharding import PartitionSpec as P

BLK = 256
TB = 2
SLOTS = 3
SIDE = BLK * TB
PARTS = 2
MESH = pl.DeviceIdType.MESH


def place():
    r, c = lax.axis_index("row"), lax.axis_index("col")
    return r // 4, c % 8, (r // 2) % 2 * 4 + c // 8, r % 2


def device(x, y, z, core):
    return (x * 4 + z // 4 * 2 + core, z % 4 * 8 + y)


def along(rows, cols):
    r, c = lax.axis_index("row"), lax.axis_index("col")
    return ((r + rows) % 32, (c + cols) % 32)


def signal(sem, target):
    pl.semaphore_signal(sem, inc=1, device_id=target, device_id_type=MESH)


def start(copies):
    for copy in copies:
        copy.start()


def halves(block):
    top = block.astype(jnp.bfloat16)
    return top, (block - top.astype(jnp.float32)).astype(jnp.bfloat16)


def densify(slots, where, high, low):
    positions = where[...]
    for p in range(TB * TB):
        r, k = p // TB, p % TB
        chosen = [(positions[:, s : s + 1] == p).astype(jnp.float32) for s in range(SLOTS)]
        block = chosen[0] * slots[0] + chosen[1] * slots[1] + chosen[2] * slots[2]
        spot = (pl.ds(r * BLK, BLK), pl.ds(k * BLK, BLK))
        high[spot], low[spot] = halves(block)


def three_dots(lh, ll, rh, rl):
    left = jnp.concatenate([lh, lh, ll], axis=1)
    right = jnp.concatenate([rh, rl, rh], axis=0)
    return jnp.dot(left, right, preferred_element_type=jnp.float32)


def kernel(
    a, a_pos, b, b_pos, out, a_own, b_own, a_in, b_in, passing, where, tiles, load, send, recv, relay, ready, ready_wrap, ready_last, ready_over, ready_next
):
    x, y, z, core = place()
    lo = z % 4
    far = core == 0
    upper = z >= 4
    barrier = pltpu.get_barrier_semaphore()

    local = [
        pltpu.make_async_copy(a, a_own, load.at[0]),
        pltpu.make_async_copy(b, b_own, load.at[1]),
        pltpu.make_async_copy(a_pos, where.at[0], load.at[2]),
        pltpu.make_async_copy(b_pos, where.at[1], load.at[3]),
    ]
    start(local)

    wrap = y == 0
    detour = jnp.where(far, 1, 2)
    aside = y == detour
    outer = y == 7
    lower = jnp.logical_not(upper)
    near = jnp.logical_not(far)
    early, late = lo == 0, lo == 3
    first = z == 0
    told = jnp.logical_and(wrap, first)
    corner = jnp.logical_and(jnp.logical_and(wrap, far), x == 0)
    zero, spared = jnp.logical_and(corner, first), jnp.logical_and(corner, z == 1)
    to_zero = jnp.logical_and(jnp.logical_and(wrap, near), jnp.logical_and(z == 4, x == 7))
    inner = jnp.logical_and(jnp.logical_or(wrap, aside), jnp.logical_not(zero))
    after_zero = jnp.logical_and(jnp.logical_and(inner, far), jnp.logical_and(z == 3, x == 0))
    indirect = jnp.logical_or(early, upper)
    direct = jnp.logical_not(indirect)
    from_zero = jnp.logical_and(jnp.logical_and(first, far), x == 0)
    handing = jnp.logical_and(jnp.logical_and(outer, indirect), jnp.logical_not(from_zero))
    end_of_zero = jnp.logical_and(jnp.logical_and(outer, far), jnp.logical_and(z == 3, x == 0))
    z_to = jnp.where(early, z + 3, z - 1)
    z_from = jnp.where(late, z - 3, z + 1)
    wrap_to = [device(x, 7, z, core), device(x, 0, z_to, core), device(x, detour, z_to, core)]
    wrap_from = device(x, 0, z_from, core)
    last = device(x, 7, z, core)
    last_to, last_from = device(x, 7, z_to, core), device(x, 7, z_from, core)
    a_to, a_from = along(0, -1), along(0, 1)
    b_to, b_from = along(-1, 0), along(1, 0)

    def remote(src, dst, ss, rs, target):
        return pltpu.make_async_remote_copy(
            src_ref=src, dst_ref=dst, send_sem=ss, recv_sem=rs, device_id=target, device_id_type=MESH
        )

    def to_slot(src, which, slot, target):
        dst = (a_in, b_in)[which].at[slot]
        return remote(src, dst, send.at[which, slot], recv.at[which, slot], target)

    a_places = remote(a_pos, where.at[2], send.at[0, SLOTS], recv.at[0, SLOTS], a_to)
    b_places = remote(b_pos, where.at[3], send.at[1, SLOTS], recv.at[1, SLOTS], b_to)
    a_sends = [to_slot(a.at[s], 0, s, a_to) for s in range(SLOTS)]
    b_sends = [to_slot(b.at[s], 1, s, b_to) for s in range(SLOTS)]

    rows = [pl.ds(i * BLK // PARTS, BLK // PARTS) for i in range(PARTS)]
    step_places = remote(a_pos, where.at[4], send.at[0, SLOTS], relay.at[2, 0], wrap_to[0])
    step = [
        [remote(a.at[s, part], passing.at[part], send.at[0, s], relay.at[0, i], wrap_to[s]) for i, part in enumerate(rows)]
        for s in range(SLOTS)
    ]
    slot = jnp.where(outer, 0, jnp.where(wrap, 1, 2))
    target = [jnp.where(outer, u, v) for u, v in zip(last_to, last)]
    pass_places = remote(where.at[4], where.at[2], relay.at[2, 1], recv.at[0, SLOTS], tuple(target))
    forward = [
        remote(passing.at[part], a_in.at[slot, part], relay.at[1, i], recv.at[0, slot], tuple(target))
        for i, part in enumerate(rows)
    ]

    @pl.when(y < 4)
    def _():
        signal(barrier, a_from)

    @pl.when(y > 4)
    def _():
        signal(barrier, a_to)

    @pl.when(jnp.logical_and(inner, jnp.logical_or(jnp.logical_not(late), after_zero)))
    def _():
        signal(barrier, wrap_from)

    @pl.when(jnp.logical_and(wrap, jnp.logical_and(early, jnp.logical_not(zero))))
    def _():
        signal(barrier, wrap_to[1])
        signal(barrier, wrap_to[2])

    @pl.when(jnp.logical_and(wrap, direct))
    def _():
        signal(barrier, last_to)

    @pl.when(jnp.logical_and(outer, jnp.logical_and(upper, jnp.logical_not(late))))
    def _():
        signal(barrier, last_from)

    @pl.when(jnp.logical_and(handing, early))
    def _():
        signal(barrier, last_to)

    @pl.when(end_of_zero)
    def _():
        signal(barrier, wrap_from)

    @pl.when(jnp.logical_and(inner, jnp.logical_not(told)))
    def _():
        signal(barrier, last)

    @pl.when(jnp.logical_and(outer, first))
    def _():
        signal(barrier, device(x, 0, z, core))

    @pl.when(jnp.logical_and(jnp.logical_or(near, lower), jnp.logical_not(zero)))
    def _():
        signal(barrier, b_to)

    @pl.when(jnp.logical_and(near, jnp.logical_or(lower, to_zero)))
    def _():
        signal(barrier, b_from)

    def count(condition, number=1):
        return jnp.where(condition, number, 0)

    replying = jnp.logical_and(y >= 4, y < 7)
    need = count(jnp.logical_and(y > 0, y < 5)) + count(replying) + count(jnp.logical_and(wrap, jnp.logical_not(early)), 2 - count(spared))
    need += count(far) + count(upper) - count(to_zero) + count(zero, 4) + count(told) - count(after_zero)
    need += count(outer, 2 - count(first) + count(z < 3) + count(late) + count(z > 4)) - count(end_of_zero)
    need += count(jnp.logical_and(inner, late))

    @pl.when(need > 0)
    def _():
        pl.semaphore_wait(barrier, need)

    @pl.when(jnp.logical_and(jnp.logical_or(far, upper), jnp.logical_not(to_zero)))
    def _():
        signal(ready, b_from)

    @pl.when(jnp.logical_and(far, jnp.logical_or(upper, zero)))
    def _():
        b_places.start()
        start(b_sends)

    @pl.when(jnp.logical_and(wrap, jnp.logical_and(late, jnp.logical_not(after_zero))))
    def _():
        signal(ready_wrap, wrap_from)

    @pl.when(jnp.logical_and(aside, jnp.logical_and(late, jnp.logical_not(after_zero))))
    def _():
        signal(ready_over, wrap_from)

    @pl.when(outer)
    def _():
        @pl.when(z > 0)
        def _():
            signal(ready_last, device(x, 0, z, core))

        signal(ready_last, device(x, detour, z, core))

        @pl.when(jnp.logical_and(late, jnp.logical_not(end_of_zero)))
        def _():
            signal(ready_wrap, last_from)

        @pl.when(z < 3)
        def _():
            signal(ready_over, wrap_from)

    @pl.when(replying)
    def _():
        signal(ready_next, a_from)

    @pl.when(y > 4)
    def _():
        pl.semaphore_wait(ready_next, 1)

    @pl.when(y > 0)
    def _():
        a_places.start()
        start(a_sends)

    def send_near():
        pl.semaphore_wait(ready, 1)
        b_places.start()
        start(b_sends)

    @pl.when(jnp.logical_and(wrap, jnp.logical_not(early)))
    def _():
        @pl.when(jnp.logical_not(spared))
        def _():
            start(step[1])

        start(step[2])

        @pl.when(upper)
        def _():
            pl.semaphore_wait(ready_last, 1)
            step_places.start()
            start(step[0])

        @pl.when(lower)
        def _():
            pl.semaphore_wait(ready_over, 1)
            a_places.start()
            a_sends[0].start()

        @pl.when(spared)
        def _():
            a_sends[1].start()

    @pl.when(jnp.logical_and(near, upper))
    def _():
        send_near()

    waiting = jnp.logical_and(wrap, z == 4)

    @pl.when(waiting)
    def _():
        for copy in a_sends[:2]:
            copy.wait_recv()

    @pl.when(jnp.logical_and(wrap, early))
    def _():
        @pl.when(z > 0)
        def _():
            pl.semaphore_wait(ready_last, 1)

        @pl.when(zero)
        def _():
            a_places.start()
            a_sends[0].start()

        @pl.when(jnp.logical_not(zero))
        def _():
            step_places.start()
            start(step[0])
            pl.semaphore_wait(ready_wrap, 1)

        start(step[1])

        @pl.when(jnp.logical_not(zero))
        def _():
            pl.semaphore_wait(ready_over, 1)

        start(step[2])

    @pl.when(jnp.logical_and(near, lower))
    def _():
        send_near()

    def pass_on():
        for one, other in zip(step[0], forward):
            one.wait_recv()
            other.start()

    def hand_on():
        @pl.when(early)
        def _():
            pl.semaphore_wait(ready_wrap, 1)

        step_places.wait_recv()
        pass_places.start()
        pass_on()

    @pl.when(jnp.logical_and(handing, z != 4))
    def _():
        hand_on()

    held_up = jnp.logical_and(jnp.logical_and(far, lower), jnp.logical_and(z >= 2, wrap))
    held_last = jnp.logical_and(jnp.logical_and(far, lower), jnp.logical_and(z >= 2, y > 0))

    @pl.when(jnp.logical_and(jnp.logical_and(far, lower), jnp.logical_not(zero)))
    def _():
        pl.semaphore_wait(ready, 1)

        @pl.when(held_up)
        def _():
            a_sends[0].wait_recv()
            a_sends[1].wait_recv()

            @pl.when(late)
            def _():
                a_sends[2].wait_recv()

        @pl.when(held_last)
        def _():
            for copy in a_sends:
                copy.wait_send()

        b_places.start()
        start(b_sends)

    @pl.when(jnp.logical_or(aside, jnp.logical_and(wrap, direct)))
    def _():
        pl.semaphore_wait(ready_last, 1)

    ah, al, bh, bl = (tiles.at[i] for i in range(4))

    def turn(i, carry):
        passing_now = (i == 0) != jnp.logical_or(late, upper)

        @pl.when(jnp.logical_and(inner, passing_now))
        def _():
            pass_on()

        @pl.when(jnp.logical_and(jnp.logical_and(handing, z == 4), passing_now))
        def _():
            hand_on()

        @pl.when(jnp.logical_not(passing_now))
        def _():
            for copy in local:
                copy.wait()
            densify(a_own, where.at[0], ah, al)
            densify(b_own, where.at[1], bh, bl)
            for c in range(TB):
                cols = pl.ds(c * BLK, BLK)
                out[:, cols] = three_dots(ah[...], al[...], bh[:, cols], bl[:, cols])

        return carry

    lax.fori_loop(0, 2, turn, 0)

    a_last = jnp.logical_and(outer, jnp.logical_or(upper, jnp.logical_and(late, far)))

    @pl.when(a_last)
    def _():
        b_places.wait_recv()
        for copy in b_sends:
            copy.wait_recv()
        densify(b_in, where.at[3], bh, bl)
        a_places.wait_recv()
        positions = where[2]
        for s in range(SLOTS):
            row = positions[:, s : s + 1] // TB
            col = positions[:, s : s + 1] % TB
            picked = [jnp.where(col == 0, t[:BLK], t[BLK:]) for t in (bh[...], bl[...])]
            a_sends[s].wait_recv()
            term = three_dots(*halves(a_in[s]), *picked)
            for r in range(TB):
                out[pl.ds(r * BLK, BLK), :] += (row == r).astype(jnp.float32) * term

    @pl.when(jnp.logical_not(a_last))
    def _():
        a_places.wait_recv()

        @pl.when(jnp.logical_not(jnp.logical_or(held_up, waiting)))
        def _():
            a_sends[0].wait_recv()
            a_sends[1].wait_recv()

        @pl.when(jnp.logical_not(jnp.logical_and(held_up, late)))
        def _():
            a_sends[2].wait_recv()

        densify(a_in, where.at[2], ah, al)
        b_places.wait_recv()
        positions = where[3]
        for s in range(SLOTS):
            row = positions[:, s : s + 1] // TB
            picked = [jnp.where(row == 0, t[:, :BLK], jnp.where(row == 1, t[:, BLK:], 0)) for t in (ah[...], al[...])]
            b_sends[s].wait_recv()
            term = three_dots(*picked, *halves(b_in[s]))
            for c in range(TB):
                here = jnp.logical_and(positions[:, s : s + 1] % TB == c, row < TB).astype(jnp.float32)
                out[:, pl.ds(c * BLK, BLK)] += here * term

    @pl.when(jnp.logical_not(held_last))
    def _():
        for copy in a_sends:
            copy.wait_send()

    for copy in [a_places, b_places] + b_sends:
        copy.wait_send()

    @pl.when(jnp.logical_or(inner, handing))
    def _():
        for copy in forward:
            copy.wait_send()

    @pl.when(handing)
    def _():
        pass_places.wait_send()


def body(a_blocks, a_positions, b_blocks, b_positions):
    held = pltpu.VMEM((SLOTS, BLK, BLK), jnp.float32)
    inputs = (a_blocks[0, 0], a_positions[0], b_blocks[0, 0], b_positions[0])
    return pl.pallas_call(
        kernel,
        out_shape=jax.ShapeDtypeStruct((SIDE, SIDE), jnp.float32),
        in_specs=[pl.BlockSpec(memory_space=pltpu.HBM)] * 4,
        out_specs=pl.BlockSpec(memory_space=pltpu.VMEM),
        scratch_shapes=[
            held,
            held,
            held,
            held,
            pltpu.VMEM((BLK, BLK), jnp.float32),
            pltpu.VMEM((5, 1, SLOTS), jnp.int32),
            pltpu.VMEM((4, SIDE, SIDE), jnp.bfloat16),
            pltpu.SemaphoreType.DMA((4,)),
            pltpu.SemaphoreType.DMA((2, SLOTS + 1)),
            pltpu.SemaphoreType.DMA((2, SLOTS + 1)),
            pltpu.SemaphoreType.DMA((3, PARTS)),
            pltpu.SemaphoreType.REGULAR,
            pltpu.SemaphoreType.REGULAR,
            pltpu.SemaphoreType.REGULAR,
            pltpu.SemaphoreType.REGULAR,
            pltpu.SemaphoreType.REGULAR,
        ],
        compiler_params=pltpu.CompilerParams(
            collective_id=0, has_side_effects=True, vmem_limit_bytes=40 * 1024 * 1024
        ),
    )(*(pltpu.with_memory_space_constraint(v, pltpu.HBM) for v in inputs))


def solution(mesh):
    placed = (
        P("row", "col", None, None, None),
        P("row", "col", None),
        P("row", "col", None, None, None),
        P("row", "col", None),
    )
    return jax.shard_map(body, mesh=mesh, in_specs=placed, out_specs=P("row", "col"), check_vma=False)
```
